128 devices in a mesh: clus: 16 (over z, y_hi, core), dir: 8 (over x, y_lo).
Axes of the slice: x: 4, y: 4 (y_hi: 2, y_lo: 2; y = y_hi * 2 + y_lo), z: 4, core: 2. Of those that a mesh axis runs over, the one named last changes fastest.
Arguments:
- currents: bfloat16 [2, 512, 64, 128], P(None, 'clus', 'dir'), may hold values from -6 to 6
- cluster_size: int32 [512], P('clus'), may hold values from 32 to 128
- radiation: bfloat16 [2, 512, 256, 128], P(None, 'clus', 'dir'), may hold values from -0.5 to 0.5
- receive: bfloat16 [2, 512, 256, 128], P(None, 'clus', 'dir'), may hold values from -0.375 to 0.375
- phase: float32 [512, 512], P('clus', 'dir'), may hold values from -3.140625 to 3.140625
- interp: float32 [8, 64, 32], P('dir'), may hold values from -1 to 1
- trans: bfloat16 [2, 256, 64, 512], P(None, 'clus', None, 'dir'), may hold values from -0.75 to 0.75
- far_ids: int32 [256, 64], P('clus'), may hold values from 0 to 255
- far_live: int32 [256, 64], P('clus'), may hold values 0 or 1
- near_blocks: bfloat16 [2, 512, 16, 128, 128], P(None, 'clus', 'dir'), may hold values from -0.125 to 0.125
- near_offset: int32 [512, 16], P('clus', 'dir'), may hold values from -32 to 32
- near_live: int32 [512, 16], P('clus', 'dir'), may hold values 0 or 1
Outputs:
- field: bfloat16 [2, 512, 64, 128], P(None, 'clus', 'dir')
The draws below stay inside these ranges and needn't reach their ends.
All inputs are finite; a program needn't handle non-finite values. No bound on the sum of `far_live` or of `near_live` on one device may be relied on, other than what follows from the above.
Results may differ from the reference program's by a relative error of at most 0.022.
Values may be sent and summed in bfloat16 or wider, within the bound.
No kernel may reach another device: no remote copies, remote signals or barrier semaphores. Data moves between devices by JAX's collectives and lax.ppermute only.
A program may use at most 128 MiB of HBM per device.

```python
import jax
import jax.numpy as jnp
from jax import lax

M = 128
K = 256
G = 32
E = 64
LIST = 64
CL_DEV = 32
NC = 512
NP = 256
K2 = 512
NG = 8
NEAR = 16


def plant(entries, rng, least, top_value):
    spot = [jax.random.randint(jax.random.fold_in(rng, axis), (), 0, length) for axis, length in enumerate(entries.shape)]
    widest = entries.shape.index(max(entries.shape))
    next_to = spot[:widest] + [(spot[widest] + 1) % entries.shape[widest]] + spot[widest + 1:]
    return entries.at[tuple(spot)].set(least).at[tuple(next_to)].set(top_value)


def steps_of(stream_key, extent, split, low, high):
    def one(position, blocks):
        steps = jax.random.uniform(jax.random.fold_in(jax.random.fold_in(stream_key, 6), position), (blocks,), jnp.float32, low / len(split), high / len(split))
        return jnp.repeat(jnp.exp(steps), extent[position] // blocks).reshape((-1,) + (1,) * (len(extent) - position - 1))

    gain = one(*split[0])
    for cut in split[1:]:
        gain = gain * one(*cut)
    return gain


def centred(own_key, shape, spread, bound, pieces=(), kind=jnp.bfloat16):
    level = steps_of(own_key, shape, pieces, -0.22, 0.18) if pieces else 1.0
    entries = jax.random.normal(own_key, shape, jnp.float32) * spread * level
    return jnp.minimum(jnp.maximum(entries, -bound), bound).astype(kind)


def setup_inputs(seed: int = 0) -> dict:
    seeds = jax.random.split(jax.random.key(seed), 13)
    return {
        "currents": centred(seeds[0], (2, NC, E, M), 1.0, 6.0, ((1, 16), (2, 8))),
        "cluster_size": plant(jax.random.randint(seeds[1], (NC,), M // 4, M + 1), jax.random.fold_in(seeds[1], 1), M // 4, M).astype(jnp.int32),
        "radiation": centred(seeds[2], (2, NC, K, M), M ** -0.5, 0.5, ((1, 16), (2, 8))),
        "receive": centred(seeds[3], (2, NC, K, M), K ** -0.5, 0.375, ((1, 16), (2, 8))),
        "phase": jnp.clip(jax.random.uniform(seeds[4], (NC, K2), jnp.float32, -3.140625, 3.140625), -3.140625, 3.140625),
        "interp": centred(seeds[5], (NG, 2 * G, G), G ** -0.5, 1.0, ((0, 8),), jnp.float32),
        "trans": centred(seeds[6], (2, NP, LIST, K2), LIST ** -0.5, 0.75, ((1, 16), (3, 8))),
        "far_ids": plant(jax.random.randint(seeds[7], (NP, LIST), 0, NP), jax.random.fold_in(seeds[7], 1), 0, NP - 1).astype(jnp.int32),
        "far_live": plant((jax.random.randint(seeds[8], (NP, LIST), 0, 4) < 3).astype(jnp.int32), jax.random.fold_in(seeds[8], 1), 0, 1),
        "near_blocks": centred(seeds[9], (2, NC, NEAR, M, M), (M * NEAR) ** -0.5, 0.125, ((1, 16), (2, 8))),
        "near_offset": plant(jax.random.randint(seeds[10], (NC, NEAR), 0 - CL_DEV, CL_DEV + 1), jax.random.fold_in(seeds[10], 1), 0 - CL_DEV, CL_DEV).astype(jnp.int32),
        "near_live": plant((jax.random.randint(seeds[11], (NC, NEAR), 0, 4) < 3).astype(jnp.int32), jax.random.fold_in(seeds[11], 1), 0, 1),
    }


def complex_einsum(formula, former, latter):
    highest = lax.Precision.HIGHEST
    former = former.astype(jnp.float32)
    latter = latter.astype(jnp.float32)

    def single(first_part, second_part):
        return jnp.einsum(formula, first_part, second_part, precision=highest)

    real_part = single(former[0], latter[0]) - single(former[1], latter[1])
    imag_part = single(former[0], latter[1]) + single(former[1], latter[0])
    return jnp.stack([real_part, imag_part])


def reference(currents, cluster_size, radiation, receive, phase, interp, trans, far_ids, far_live, near_blocks, near_offset, near_live):
    highest = lax.Precision.HIGHEST
    alive_mask = jnp.arange(M, dtype=jnp.int32)[None, :] < cluster_size[:, None]
    masked = jnp.where(alive_mask[None, :, None, :], currents, jnp.zeros((), currents.dtype))
    spectra = complex_einsum("ckm,cem->cke", radiation, masked)
    grouped = spectra.reshape(2, NC, NG, G, E)
    raised = jnp.einsum("ghk,rcgke->rcghe", interp, grouped, precision=highest).reshape(2, NC, K2, E)
    cosine = jnp.cos(phase)[:, :, None]
    sine = jnp.sin(phase)[:, :, None]
    shifted = jnp.stack([cosine * raised[0] - sine * raised[1], sine * raised[0] + cosine * raised[1]])
    parents = jnp.sum(shifted.reshape(2, NP, 2, K2, E), axis=2).astype(jnp.bfloat16)

    def translate_entry(entry, accum):
        targets = lax.dynamic_index_in_dim(far_ids, entry, 1, keepdims=False)
        sources = jnp.take(parents, targets, axis=1).astype(jnp.float32)
        factor = lax.dynamic_index_in_dim(trans, entry, 2, keepdims=False).astype(jnp.float32)
        enabled = lax.dynamic_index_in_dim(far_live, entry, 1, keepdims=False).astype(jnp.float32)[:, None, None]
        real_w = factor[0][:, :, None] * enabled
        imag_w = factor[1][:, :, None] * enabled
        return accum + jnp.stack([real_w * sources[0] - imag_w * sources[1], real_w * sources[1] + imag_w * sources[0]])

    translated = lax.fori_loop(0, LIST, translate_entry, jnp.zeros((2, NP, K2, E), jnp.float32)).astype(jnp.bfloat16)
    twice = jnp.repeat(translated.astype(jnp.float32), 2, axis=1)
    downward = jnp.stack([cosine * twice[0] + sine * twice[1], cosine * twice[1] - sine * twice[0]])
    lowered = jnp.einsum("ghk,rcghe->rcgke", interp, downward.reshape(2, NC, NG, 2 * G, E), precision=highest)
    lowered = lowered.reshape(2, NC, K, E).astype(jnp.bfloat16)
    far_field = complex_einsum("cke,ckm->cem", lowered, receive)
    source_ids = jnp.clip(jnp.arange(NC, dtype=jnp.int32)[:, None] + near_offset, 0, NC - 1).astype(jnp.int32)

    def near_entry(entry, accum):
        column = lax.dynamic_index_in_dim(source_ids, entry, 1, keepdims=False)
        picked = jnp.take(masked, column, axis=1)
        enabled = lax.dynamic_index_in_dim(near_live, entry, 1, keepdims=False)
        picked = jnp.where(enabled[None, :, None, None] == 1, picked, jnp.zeros((), picked.dtype))
        blocks = lax.dynamic_index_in_dim(near_blocks, entry, 2, keepdims=False)
        return accum + complex_einsum("cmn,cen->cem", blocks, picked)

    near_field = lax.fori_loop(0, NEAR, near_entry, jnp.zeros((2, NC, E, M), jnp.float32))
    summed = far_field + near_field
    return jnp.where(alive_mask[None, :, None, :], summed, jnp.zeros((), summed.dtype)).astype(jnp.bfloat16)
```

```python
import jax
import jax.numpy as jnp
from jax import lax
from jax.experimental import pallas as pl
from jax.experimental.pallas import tpu as pltpu
from jax.sharding import PartitionSpec as P

BF = jnp.bfloat16
F32 = jnp.float32
NT = (((1,), (1,)), ((), ()))
NN = (((1,), (0,)), ((), ()))
TN = (((0,), (0,)), ((), ()))
VMEM = pl.BlockSpec(memory_space=pltpu.VMEM)
SMEM = pl.BlockSpec(memory_space=pltpu.SMEM)


def dot(a, b, dims):
    return lax.dot_general(a, b, dims, preferred_element_type=F32)


def params(mib):
    return pltpu.CompilerParams(vmem_limit_bytes=mib * 2**20)


def turn_lanes(x):
    lane = lax.broadcasted_iota(jnp.int32, x.shape, 1)
    return jnp.where(lane % 16 < 8, -pltpu.roll(x, 120, 1), pltpu.roll(x, 8, 1))


def turn_rows(x):
    y = x.reshape(8, 2, 8, x.shape[1])
    return jnp.stack([-y[:, 1], y[:, 0]], axis=1).reshape(x.shape)


def pack_kernel(trans, live, ids, out, rows):
    for pp in range(8):
        for r in range(2):
            tiles = []
            for p in (2 * pp, 2 * pp + 1):
                tile = trans[r, p].astype(F32).T
                tiles.append(jnp.where(live[pl.ds(p, 1), :] == 1, tile, 0.0))
            rows[pl.ds(r * 8 + pp, 64, stride=16), :] = jnp.concatenate(tiles, axis=1)
    out[:, 0:64, :] = rows[...].reshape(16, 64, 128).astype(BF)
    pairs = ids[...].astype(F32)
    pairs = jnp.concatenate([pairs, jnp.zeros((8, 128), F32)], axis=0).astype(BF)
    out[:, 64:80, :] = jnp.broadcast_to(pairs[None], (16, 16, 128))


def weights_kernel(packed, out, rows, ids, sums):
    rows[...] = packed[:, 0:64, :].astype(F32).reshape(1024, 128)
    ids[...] = packed[:, 64:80, :].astype(F32)[:, 0:8, :].reshape(128, 128).astype(jnp.int32)
    lane = lax.broadcasted_iota(jnp.int32, (8, 128), 1)
    source = lax.broadcasted_iota(jnp.int32, (256, 128), 0)

    def step(i, carry):
        factors = rows[pl.ds((i // 8) * 64 + i % 8, 8, stride=8), :]
        left = jnp.concatenate(
            [jnp.where(lane < 64, factors, 0.0), jnp.where(lane < 64, 0.0, factors)], axis=0
        ).astype(BF)
        hit = jnp.where(source == ids[pl.ds(i, 1), :], 1.0, 0.0).astype(BF)
        made = dot(left, hit, NT)
        for b in range(2):
            for h in range(2):
                sums[h, pl.ds(2 * i + b, 8, stride=256), :] = made[
                    b * 8 : b * 8 + 8, h * 128 : h * 128 + 128
                ]
        return carry

    lax.fori_loop(0, 128, step, 0, unroll=8)
    out[...] = sums[...].astype(BF)


def fold_kernel(radiation, receive, phase, interp4, up, down):
    cosine = jnp.cos(phase[...])
    sine = jnp.sin(phase[...])
    raise4 = interp4[...].astype(BF)
    for g in range(8):
        sent = [dot(raise4, radiation[r, g * 4 : g * 4 + 4].reshape(128, 128), NN) for r in range(2)]
        got = [dot(raise4, receive[r, g * 4 : g * 4 + 4].reshape(128, 128), NN) for r in range(2)]
        for n in range(4):
            c = g * 4 + n
            co = jnp.broadcast_to(cosine[:, c : c + 1], (64, 128))
            si = jnp.broadcast_to(sine[:, c : c + 1], (64, 128))
            ur, ui = (s[n * 64 : n * 64 + 64] for s in sent)
            vr, vi = (s[n * 64 : n * 64 + 64] for s in got)
            b = (c % 2) * 128
            up[c // 2, 0:64, b : b + 128] = (co * ur - si * ui).astype(BF)
            up[c // 2, 64:128, b : b + 128] = (si * ur + co * ui).astype(BF)
            down[c, :, 0:128] = (co * vr + si * vi).astype(BF)
            down[c, :, 128:256] = (co * vi - si * vr).astype(BF)


def parents_kernel(everyone, up, out, rows):
    for p in range(16):
        x = jnp.concatenate(
            [everyone[:, 2 * p + b].reshape(128, 128) for b in range(2)], axis=1
        )
        y = dot(up[p], x, NT)
        rows[pl.ds(p, 64, stride=16), :] = y[0:64] + turn_lanes(y[64:128])
    out[...] = rows[...].reshape(16, 64, 128).astype(BF)


def translate_kernel(sources, weights, out):
    for q in range(4):
        src = sources[:, q * 16 : q * 16 + 16, :].reshape(256, 128)
        w = slice(q * 512, q * 512 + 512)
        z = dot(weights[0, w, :], src[0:128], NN) + dot(weights[1, w, :], src[128:256], NN)
        done = z[0:256] + turn_lanes(z[256:512])
        out[:, q * 16 : q * 16 + 16, :] = done.reshape(16, 16, 128).astype(BF)


def near_kernel(place, offset, live, own, partner, far, blocks, out, cells):
    first = place[0] * 32
    even = place[0] % 2 == 0
    cells[:, 32:64] = own[...]
    cells[:, pl.ds(jnp.where(even, 64, 0), 32)] = partner[...]
    cells[:, pl.ds(jnp.where(even, 0, 64), 32)] = far[...]
    last = place[1] * 32 - 1

    def step(c, carry):
        total = [jnp.zeros((128, 128), F32), jnp.zeros((128, 128), F32)]
        for j in range(2):
            source = jnp.clip(first + c + offset[c, j], 0, last) - first + 32
            x = cells[:, source].reshape(128, 128)
            x = jnp.where(live[c, j] == 1, x, jnp.zeros_like(x))
            for r in range(2):
                total[r] += dot(x, blocks[r, c, j], NT)
        out[c] = (total[0] + turn_rows(total[1])).astype(BF)
        return carry

    lax.fori_loop(0, 32, step, 0, unroll=4)


def far_kernel(translated, down, near, out, rows):
    rows[...] = translated[...].astype(F32).reshape(1024, 128)
    for p in range(16):
        t = rows[pl.ds(p, 64, stride=16), :].T.astype(BF)
        for c in (2 * p, 2 * p + 1):
            y = dot(t, down[c], NN)
            field = y[:, 0:128] + turn_rows(y[:, 128:256]) + near[c].astype(F32)
            out[:, c] = field.reshape(8, 16, 128).astype(BF)


def call(kernel, shape, scratch, mib, specs, cost, dtype=BF):
    many = isinstance(shape, list)
    outs = [jax.ShapeDtypeStruct(s, dtype) for s in (shape if many else [shape])]
    return pl.pallas_call(
        kernel,
        out_shape=outs if many else outs[0],
        in_specs=specs,
        out_specs=[VMEM] * len(outs) if many else VMEM,
        scratch_shapes=scratch,
        compiler_params=params(mib),
        cost_estimate=pl.CostEstimate(flops=cost[0], bytes_accessed=cost[1], transcendentals=0),
    )


def local(
    currents,
    cluster_size,
    radiation,
    receive,
    phase,
    interp,
    trans,
    far_ids,
    far_live,
    near_blocks,
    near_offset,
    near_live,
):
    place = lax.axis_index("clus")
    count = lax.axis_size("clus")
    alive = lax.broadcasted_iota(jnp.int32, (32, 128), 1) < cluster_size[:, None]

    packed = call(
        pack_kernel, (16, 80, 128), [pltpu.VMEM((1024, 128), F32)], 16, [VMEM] * 3, (1, 2**20)
    )(trans, far_live, far_ids.reshape(8, 128))
    packed = lax.all_to_all(packed, "clus", 0, 0)

    masked = jnp.where(alive[None, :, None, :], currents, jnp.zeros((), BF))
    masked = masked.transpose(1, 0, 2, 3).reshape(1, 32, 16, 128)
    everyone = lax.all_to_all(jnp.broadcast_to(masked, (8, 32, 16, 128)), "dir", 0, 0)

    weights = call(
        weights_kernel,
        (2, 2048, 128),
        [
            pltpu.VMEM((1024, 128), F32),
            pltpu.VMEM((128, 128), jnp.int32),
            pltpu.VMEM((2, 2048, 128), F32),
        ],
        24,
        [VMEM],
        (2**32, 2**23),
    )(packed)
    interp4 = jnp.kron(jnp.eye(4, dtype=F32), interp[0])
    up, down = call(
        fold_kernel, [(16, 128, 256), (32, 64, 256)], [], 24, [VMEM] * 4, (2**31, 2**23)
    )(radiation, receive, phase.T, interp4)

    rows = pltpu.VMEM((1024, 128), F32)
    parents = call(parents_kernel, (16, 64, 128), [rows], 24, [VMEM] * 2, (2**27, 2**21))(
        everyone, up
    )
    partner = lax.ppermute(everyone, "clus", [(i, i ^ 1) for i in range(count)])
    across = [(i, i + 1) for i in range(1, count - 1, 2)]
    far = lax.ppermute(everyone, "clus", across + [(b, a) for a, b in across])
    sources = lax.all_to_all(parents, "clus", 0, 0)
    translated = call(translate_kernel, (16, 64, 128), [], 24, [VMEM] * 2, (2**28, 2**21))(
        sources, weights
    )
    back = lax.all_to_all(translated, "clus", 0, 0)
    near = call(
        near_kernel,
        (32, 128, 128),
        [pltpu.VMEM((8, 96, 16, 128), BF)],
        32,
        [SMEM] * 3 + [VMEM] * 4,
        (2**32, 2**23),
    )(jnp.stack([place, count]).astype(jnp.int32), near_offset, near_live, everyone, partner, far, near_blocks)
    partial = call(far_kernel, (8, 32, 16, 128), [rows], 24, [VMEM] * 3, (2**28, 2**22))(
        back, down, near
    )
    shares = lax.all_to_all(partial, "dir", 0, 0)
    field = jnp.sum(shares.astype(F32), axis=0).reshape(32, 2, 8, 128)
    field = jnp.where(alive[:, None, None, :], field, 0.0).astype(BF)
    return field.transpose(1, 0, 2, 3)


def solution(mesh):
    in_specs = (
        P(None, "clus", "dir", None),
        P("clus"),
        P(None, "clus", "dir", None),
        P(None, "clus", "dir", None),
        P("clus", "dir"),
        P("dir", None, None),
        P(None, "clus", None, "dir"),
        P("clus", None),
        P("clus", None),
        P(None, "clus", "dir", None, None),
        P("clus", "dir"),
        P("clus", "dir"),
    )
    out_specs = P(None, "clus", "dir", None)
    return jax.shard_map(local, mesh=mesh, in_specs=in_specs, out_specs=out_specs, check_vma=False)
```

```python
import jax
import jax.numpy as jnp
from jax import lax
from jax.experimental import pallas as pl
from jax.experimental.pallas import tpu as pltpu
from jax.sharding import PartitionSpec as P

BF = jnp.bfloat16
F32 = jnp.float32
NT = (((1,), (1,)), ((), ()))
NN = (((1,), (0,)), ((), ()))
TN = (((0,), (0,)), ((), ()))
VMEM = pl.BlockSpec(memory_space=pltpu.VMEM)
ANY = pl.BlockSpec(memory_space=pl.ANY)
SMEM = pl.BlockSpec(memory_space=pltpu.SMEM)


def dot(a, b, dims):
    return lax.dot_general(a, b, dims, preferred_element_type=F32)


def params(mib):
    return pltpu.CompilerParams(vmem_limit_bytes=mib * 2**20)


def turn_lanes(x):
    lane = lax.broadcasted_iota(jnp.int32, x.shape, 1)
    return jnp.where(lane % 16 < 8, -pltpu.roll(x, 120, 1), pltpu.roll(x, 8, 1))


def turn_rows(x):
    y = x.reshape(8, 2, 8, x.shape[1])
    return jnp.stack([-y[:, 1], y[:, 0]], axis=1).reshape(x.shape)


def mask_kernel(size, currents, copies, own, alive):
    lane = lax.broadcasted_iota(jnp.int32, (16, 128), 1)
    for c in range(32):
        both = jnp.concatenate([currents[0, c], currents[1, c]], axis=0).astype(F32)
        alive[c] = jnp.where(lane < size[c], 1.0, 0.0)
        both = jnp.where(lane < size[c], both, 0.0).astype(BF)
        own[c] = both
        for d in range(8):
            copies[d, c] = both


def pack_kernel(trans, live, ids, out, rows):
    for pp in range(8):
        for r in range(2):
            tiles = []
            for p in (2 * pp, 2 * pp + 1):
                tile = trans[r, p].astype(F32).T
                tiles.append(jnp.where(live[pl.ds(p, 1), :] == 1, tile, 0.0))
            rows[pl.ds(r * 8 + pp, 64, stride=16), :] = jnp.concatenate(tiles, axis=1)
    out[:, 0:64, :] = rows[...].reshape(16, 64, 128).astype(BF)
    pairs = ids[...].astype(F32)
    pairs = jnp.concatenate([pairs, jnp.zeros((8, 128), F32)], axis=0).astype(BF)
    out[:, 64:80, :] = jnp.broadcast_to(pairs[None], (16, 16, 128))


def weights_kernel(packed, out, rows, ids, sums):
    rows[...] = packed[:, 64:128, :].astype(F32).reshape(1024, 128)
    ids[...] = packed[:, 128:144, :].astype(F32)[:, 0:8, :].reshape(128, 128)
    lane = lax.broadcasted_iota(jnp.int32, (8, 128), 1)
    source = lax.broadcasted_iota(jnp.int32, (256, 128), 0).astype(BF)
    none = jnp.zeros((16, 128), BF)

    def step(i, carry):
        left, hits = [], []
        for n in range(2):
            k = 2 * i + n
            factors = rows[pl.ds((k // 8) * 64 + k % 8, 8, stride=8), :]
            both = jnp.concatenate(
                [jnp.where(lane < 64, factors, 0.0), jnp.where(lane < 64, 0.0, factors)], axis=0
            ).astype(BF)
            left.append(jnp.concatenate([none] * n + [both] + [none] * (1 - n), axis=1))
            hit = source == jnp.broadcast_to(ids[pl.ds(k, 1), :].astype(BF), (256, 128))
            hits.append(jnp.where(hit, jnp.ones((), BF), jnp.zeros((), BF)))
        made = dot(jnp.concatenate(left, axis=0), jnp.concatenate(hits, axis=1), NT)
        for b in range(4):
            for h in range(2):
                sums[h, pl.ds(4 * i + b, 8, stride=256), :] = made[
                    b * 8 : b * 8 + 8, h * 128 : h * 128 + 128
                ]
        return carry

    lax.fori_loop(0, 64, step, 0, unroll=8)
    out[...] = sums[...].astype(BF)


def fold_kernel(radiation, receive, phase, interp, up, down):
    turned = jnp.concatenate([phase[...], jnp.zeros((32, 64), F32)], axis=1).T[0:64]
    cosine = jnp.cos(turned)
    sine = jnp.sin(turned)
    raise4 = []
    for n in range(4):
        left = [jnp.zeros((32, 64 * n), F32)] if n else []
        right = [jnp.zeros((32, 64 * (3 - n)), F32)] if n < 3 else []
        raise4.append(jnp.concatenate(left + [interp[...]] + right, axis=1))
    raise4 = jnp.concatenate(raise4, axis=0).T.astype(BF)
    for g in range(8):
        sent = [dot(raise4, radiation[r, g * 4 : g * 4 + 4].reshape(128, 128), NN) for r in range(2)]
        got = [dot(raise4, receive[r, g * 4 : g * 4 + 4].reshape(128, 128), NN) for r in range(2)]
        for n in range(4):
            c = g * 4 + n
            co = jnp.broadcast_to(cosine[:, c : c + 1], (64, 128))
            si = jnp.broadcast_to(sine[:, c : c + 1], (64, 128))
            ur, ui = (s[n * 64 : n * 64 + 64] for s in sent)
            vr, vi = (s[n * 64 : n * 64 + 64] for s in got)
            b = (c % 2) * 128
            up[c // 2, 0:64, b : b + 128] = (co * ur - si * ui).astype(BF)
            up[c // 2, 64:128, b : b + 128] = (si * ur + co * ui).astype(BF)
            down[c, :, 0:128] = (co * vr + si * vi).astype(BF)
            down[c, :, 128:256] = (co * vi - si * vr).astype(BF)


def parents_kernel(everyone, up, packed, out, rows):
    out[:, 64:144, :] = packed[...]
    for p in range(16):
        x = jnp.concatenate(
            [everyone[:, 2 * p + b].reshape(128, 128) for b in range(2)], axis=1
        )
        y = dot(up[p], x, NT)
        rows[pl.ds(p, 64, stride=16), :] = y[0:64] + turn_lanes(y[64:128])
    out[:, 0:64, :] = rows[...].reshape(16, 64, 128).astype(BF)


def translate_kernel(sources, weights, out):
    for q in range(4):
        src = sources[:, q * 16 : q * 16 + 16, :].reshape(256, 128)
        w = slice(q * 512, q * 512 + 512)
        z = dot(weights[0, w, :], src[0:128], NN) + dot(weights[1, w, :], src[128:256], NN)
        done = z[0:256] + turn_lanes(z[256:512])
        out[:, q * 16 : q * 16 + 16, :] = done.reshape(16, 16, 128).astype(BF)


def near_kernel(place, offset, live, own, partner, far0, far1, far2, far3, blocks, out, far):
    first = place[0] * 32
    even = place[0] % 2 == 0
    bases = (first, jnp.where(even, first + 32, first - 32), jnp.where(even, first - 32, first + 32))
    for k, part in enumerate((far0, far1, far2, far3)):
        for b in range(2):
            far[2 * ((place[2] // 2 + 4 - k) % 4) + (place[2] + b) % 2] = part[b]

    def step(c, carry):
        picked = []
        for j in range(2):
            source = jnp.clip(first + c + offset[c, j], 0, place[1] * 32 - 1)
            x = jnp.zeros((128, 128), BF)
            for cells, base in zip((own, partner, far), bases):
                spot = source - base
                here = (live[c, j] == 1) & (spot >= 0) & (spot < 32)
                x = jnp.where(here, cells[:, jnp.clip(spot, 0, 31)].reshape(128, 128), x)
            picked.append(x)
        parts = [jnp.concatenate([blocks[r, c, j] for j in range(2)], axis=1) for r in range(2)]
        y = dot(jnp.concatenate(picked, axis=1), jnp.concatenate(parts, axis=0), NT)
        out[c] = (y[:, 0:128] + turn_rows(y[:, 128:256])).astype(BF)
        return carry

    lax.fori_loop(0, 32, step, 0, unroll=4)


def far_kernel(translated, down, near, out, rows):
    rows[...] = translated[...].astype(F32).reshape(1024, 128)
    for p in range(16):
        t = rows[pl.ds(p, 64, stride=16), :].T.astype(BF)
        for c in (2 * p, 2 * p + 1):
            y = dot(t, down[c], NN)
            field = y[:, 0:128] + turn_rows(y[:, 128:256]) + near[c].astype(F32)
            out[:, c] = field.reshape(8, 16, 128).astype(BF)


def total_kernel(shares, alive, out):
    total = shares[0].astype(F32)
    for d in range(1, 8):
        total += shares[d].astype(F32)
    total = jnp.where(alive[...] > 0.0, total, 0.0)
    for r in range(2):
        out[r] = total[:, r * 8 : r * 8 + 8].astype(BF)


def call(kernel, shape, scratch, mib, specs, cost, dtype=BF, alias={}):
    many = isinstance(shape, list)
    shapes = shape if many else [shape]
    types = dtype if isinstance(dtype, tuple) else (dtype,) * len(shapes)
    outs = [jax.ShapeDtypeStruct(s, d) for s, d in zip(shapes, types)]
    return pl.pallas_call(
        kernel,
        out_shape=outs if many else outs[0],
        in_specs=specs,
        out_specs=[VMEM] * len(outs) if many else VMEM,
        scratch_shapes=scratch,
        compiler_params=params(mib),
        input_output_aliases=alias,
        cost_estimate=pl.CostEstimate(flops=cost[0], bytes_accessed=cost[1], transcendentals=0),
    )


def local(
    currents,
    cluster_size,
    radiation,
    receive,
    phase,
    interp,
    trans,
    far_ids,
    far_live,
    near_blocks,
    near_offset,
    near_live,
):
    place = lax.axis_index("clus")
    count = lax.axis_size("clus")

    packed = call(
        pack_kernel, (16, 80, 128), [pltpu.VMEM((1024, 128), F32)], 8, [VMEM] * 3, (1, 2**20)
    )(trans, far_live, far_ids.reshape(8, 128))

    alive = lax.broadcasted_iota(jnp.int32, (32, 128), 1) < cluster_size[:, None]
    own = jnp.where(alive[None, :, None, :], currents, jnp.zeros((), BF))
    own = own.transpose(1, 0, 2, 3).reshape(1, 32, 16, 128)
    copies = jnp.broadcast_to(own, (8, 32, 16, 128))
    alive = jnp.broadcast_to(alive[:, None, :].astype(F32), (32, 16, 128))
    everyone = lax.all_to_all(copies, "dir", 0, 0)
    across = [(i, i + 1) for i in range(1, count - 1, 2)]
    across = across + [(b, a) for a, b in across]
    own = own.reshape(32, 16, 128)
    met = [
        lax.ppermute(own, ("clus", "dir"), [(a * 8 + i, b * 8 + (i ^ k)) for a, b in across for i in range(8)])
        for k in range(2)
    ]

    up, down = call(
        fold_kernel, [(16, 128, 256), (32, 64, 256)], [], 12, [VMEM] * 4, (2**31, 2**23)
    )(radiation, receive, phase, interp[0].T)

    everyone, up, down, packed = lax.optimization_barrier((everyone, up, down, packed))
    rows = pltpu.VMEM((1024, 128), F32)
    parents = call(parents_kernel, (16, 144, 128), [rows], 12, [VMEM] * 3, (2**27, 2**21))(
        everyone, up, packed
    )
    partner = lax.ppermute(everyone, "clus", [(i, i ^ 1) for i in range(count)])
    parents, met = lax.optimization_barrier((parents, met))
    far0 = jnp.stack(met)
    far1, far2, far3 = (
        lax.ppermute(far0, "dir", [(i, (i + 2 * k) % 8) for i in range(8)]) for k in (1, 2, 3)
    )
    sources = lax.all_to_all(parents, "clus", 0, 0)
    weights = call(
        weights_kernel,
        (2, 2048, 128),
        [
            pltpu.VMEM((1024, 128), F32),
            pltpu.VMEM((128, 128), F32),
            pltpu.VMEM((2, 2048, 128), F32),
        ],
        12,
        [VMEM],
        (2**32, 2**23),
    )(sources)
    translated = call(translate_kernel, (16, 64, 128), [], 12, [VMEM] * 2, (2**28, 2**21))(
        sources, weights
    )
    back = lax.all_to_all(translated, "clus", 0, 0)
    spots = jnp.stack([place, count, lax.axis_index("dir")]).astype(jnp.int32)
    near = call(
        near_kernel,
        (32, 128, 128),
        [pltpu.VMEM((8, 32, 16, 128), BF)],
        12,
        [SMEM] * 3 + [VMEM] * 7,
        (2**30, 2**23),
    )(spots, near_offset, near_live, everyone, partner, far0, far1, far2, far3, near_blocks)
    partial = call(far_kernel, (8, 32, 16, 128), [rows], 12, [VMEM] * 3, (2**28, 2**22))(
        back, down, near
    )
    shares = lax.all_to_all(partial, "dir", 0, 0)
    return call(total_kernel, (2, 32, 8, 128), [], 8, [VMEM] * 2, (1, 2**21))(shares, alive)


def solution(mesh):
    in_specs = (
        P(None, "clus", "dir", None),
        P("clus"),
        P(None, "clus", "dir", None),
        P(None, "clus", "dir", None),
        P("clus", "dir"),
        P("dir", None, None),
        P(None, "clus", None, "dir"),
        P("clus", None),
        P("clus", None),
        P(None, "clus", "dir", None, None),
        P("clus", "dir"),
        P("clus", "dir"),
    )
    out_specs = P(None, "clus", "dir", None)
    return jax.shard_map(local, mesh=mesh, in_specs=in_specs, out_specs=out_specs, check_vma=False)
```

```python
import jax
import jax.numpy as jnp
from jax import lax
from jax.experimental import pallas as pl
from jax.experimental.pallas import tpu as pltpu
from jax.sharding import PartitionSpec as P

BF = jnp.bfloat16
F32 = jnp.float32
NT = (((1,), (1,)), ((), ()))
NN = (((1,), (0,)), ((), ()))
TN = (((0,), (0,)), ((), ()))
VMEM = pl.BlockSpec(memory_space=pltpu.VMEM)
ANY = pl.BlockSpec(memory_space=pl.ANY)
SMEM = pl.BlockSpec(memory_space=pltpu.SMEM)


def dot(a, b, dims):
    return lax.dot_general(a, b, dims, preferred_element_type=F32)


def params(mib):
    return pltpu.CompilerParams(vmem_limit_bytes=mib * 2**20)


def turn_lanes(x):
    lane = lax.broadcasted_iota(jnp.int32, x.shape, 1)
    return jnp.where(lane % 16 < 8, -pltpu.roll(x, 120, 1), pltpu.roll(x, 8, 1))


def turn_rows(x):
    y = x.reshape(8, 2, 8, x.shape[1])
    return jnp.stack([-y[:, 1], y[:, 0]], axis=1).reshape(x.shape)


def mask_kernel(size, currents, copies, own, alive):
    lane = lax.broadcasted_iota(jnp.int32, (16, 128), 1)
    for c in range(32):
        both = jnp.concatenate([currents[0, c], currents[1, c]], axis=0).astype(F32)
        alive[c] = jnp.where(lane < size[c], 1.0, 0.0)
        both = jnp.where(lane < size[c], both, 0.0).astype(BF)
        own[c] = both
        for d in range(8):
            copies[d, c] = both


def pack_kernel(trans, live, ids, out, rows):
    for pp in range(8):
        for r in range(2):
            tiles = []
            for p in (2 * pp, 2 * pp + 1):
                tile = trans[r, p].astype(F32).T
                tiles.append(jnp.where(live[pl.ds(p, 1), :] == 1, tile, 0.0))
            rows[pl.ds(r * 8 + pp, 64, stride=16), :] = jnp.concatenate(tiles, axis=1)
    out[:, 0:64, :] = rows[...].reshape(16, 64, 128).astype(BF)
    pairs = ids[...].astype(F32)
    pairs = jnp.concatenate([pairs, jnp.zeros((8, 128), F32)], axis=0).astype(BF)
    out[:, 64:80, :] = jnp.broadcast_to(pairs[None], (16, 16, 128))


def translate_kernel(packed, out, rows, ids, sums):
    rows[...] = packed[:, 64:128, :].astype(F32).reshape(1024, 128)
    ids[...] = packed[:, 128:144, :].astype(F32)[:, 0:8, :].reshape(128, 128)
    lane = lax.broadcasted_iota(jnp.int32, (8, 128), 1)
    source = lax.broadcasted_iota(jnp.int32, (128, 128), 1).astype(F32)
    columns = ids[...].T
    none = jnp.zeros((16, 128), BF)
    for i in range(64):
        left, hits = [], []
        for n in range(2):
            k = 2 * i + n
            factors = rows[pl.ds((k // 8) * 64 + k % 8, 8, stride=8), :]
            both = jnp.concatenate(
                [jnp.where(lane < 64, factors, 0.0), jnp.where(lane < 64, 0.0, factors)], axis=0
            ).astype(BF)
            left.append(jnp.concatenate([none] * n + [both] + [none] * (1 - n), axis=1))
            wanted = jnp.broadcast_to(columns[:, k : k + 1], (128, 128))
            halves = [jnp.where(source == wanted - 128.0 * h, 1.0, 0.0).astype(BF) for h in range(2)]
            hits.append(jnp.concatenate(halves, axis=1))
        made = dot(jnp.concatenate(left, axis=0), jnp.concatenate(hits, axis=0), NN)
        for b in range(4):
            for h in range(2):
                sums[h, pl.ds(4 * i + b, 8, stride=256), :] = made[
                    b * 8 : b * 8 + 8, h * 128 : h * 128 + 128
                ]
    for q in range(4):
        src = packed[:, q * 16 : q * 16 + 16, :].reshape(256, 128)
        w = slice(q * 512, q * 512 + 512)
        z = dot(sums[0, w, :].astype(BF), src[0:128], NN) + dot(sums[1, w, :].astype(BF), src[128:256], NN)
        done = z[0:256] + turn_lanes(z[256:512])
        out[:, q * 16 : q * 16 + 16, :] = done.reshape(16, 16, 128).astype(BF)


def fold_kernel(patterns, phase, interp, up, down):
    turned = jnp.concatenate([phase[...], jnp.zeros((32, 64), F32)], axis=1).T[0:64]
    cosine = jnp.cos(turned)
    sine = jnp.sin(turned)
    raise4 = []
    for n in range(4):
        left = [jnp.zeros((32, 64 * n), F32)] if n else []
        right = [jnp.zeros((32, 64 * (3 - n)), F32)] if n < 3 else []
        raise4.append(jnp.concatenate(left + [interp[...]] + right, axis=1))
    raise4 = jnp.concatenate(raise4, axis=0).T.astype(BF)
    for g in range(8):
        sent = [dot(raise4, patterns[0, r, g * 4 : g * 4 + 4].reshape(128, 128), NN) for r in range(2)]
        got = [dot(raise4, patterns[1, r, g * 4 : g * 4 + 4].reshape(128, 128), NN) for r in range(2)]
        for n in range(4):
            c = g * 4 + n
            co = jnp.broadcast_to(cosine[:, c : c + 1], (64, 128))
            si = jnp.broadcast_to(sine[:, c : c + 1], (64, 128))
            ur, ui = (s[n * 64 : n * 64 + 64] for s in sent)
            vr, vi = (s[n * 64 : n * 64 + 64] for s in got)
            b = (c % 2) * 128
            up[c // 2, 0:64, b : b + 128] = (co * ur - si * ui).astype(BF)
            up[c // 2, 64:128, b : b + 128] = (si * ur + co * ui).astype(BF)
            down[c, :, 0:128] = (co * vr + si * vi).astype(BF)
            down[c, :, 128:256] = (co * vi - si * vr).astype(BF)


def pair_kernel(first, second, out):
    out[0] = first[...]
    out[1] = second[...]


def parents_kernel(everyone, up, packed, out, rows):
    out[:, 64:144, :] = packed[...]
    for p in range(16):
        x = jnp.concatenate(
            [everyone[:, 2 * p + b].reshape(128, 128) for b in range(2)], axis=1
        )
        y = dot(up[p], x, NT)
        rows[pl.ds(p, 64, stride=16), :] = y[0:64] + turn_lanes(y[64:128])
    out[:, 0:64, :] = rows[...].reshape(16, 64, 128).astype(BF)


def near_kernel(place, offset, live, own, partner, far0, far1, far2, far3, blocks, out, far):
    first = place[0] * 32
    even = place[0] % 2 == 0
    bases = (first, jnp.where(even, first + 32, first - 32), jnp.where(even, first - 32, first + 32))
    for k, part in enumerate((far0, far1, far2, far3)):
        for b in range(2):
            far[2 * ((place[2] // 2 + 4 - k) % 4) + (place[2] + b) % 2] = part[b]

    def step(c, carry):
        picked = []
        for j in range(2):
            source = jnp.clip(first + c + offset[j, c], 0, place[1] * 32 - 1)
            x = jnp.zeros((128, 128), BF)
            for cells, base in zip((own, partner, far), bases):
                spot = source - base
                here = (live[j, c] == 1) & (spot >= 0) & (spot < 32)
                x = jnp.where(here, cells[:, jnp.clip(spot, 0, 31)].reshape(128, 128), x)
            picked.append(x)
        parts = [jnp.concatenate([blocks[r, c, j] for j in range(2)], axis=1) for r in range(2)]
        y = dot(jnp.concatenate(picked, axis=1), jnp.concatenate(parts, axis=0), NT)
        out[c] = (y[:, 0:128] + turn_rows(y[:, 128:256])).astype(BF)
        return carry

    lax.fori_loop(0, 32, step, 0, unroll=4)


def far_kernel(translated, down, near, out, rows):
    rows[...] = translated[...].astype(F32).reshape(1024, 128)
    for p in range(16):
        t = rows[pl.ds(p, 64, stride=16), :].T.astype(BF)
        for c in (2 * p, 2 * p + 1):
            y = dot(t, down[c], NN)
            field = y[:, 0:128] + turn_rows(y[:, 128:256]) + near[c].astype(F32)
            out[:, c] = field.reshape(8, 16, 128).astype(BF)


def total_kernel(shares, alive, out):
    total = shares[0].astype(F32)
    for d in range(1, 8):
        total += shares[d].astype(F32)
    total = jnp.where(alive[...] > 0.0, total, 0.0)
    for r in range(2):
        out[r] = total[:, r * 8 : r * 8 + 8].astype(BF)


def call(kernel, shape, scratch, mib, specs, cost, dtype=BF, alias={}):
    many = isinstance(shape, list)
    shapes = shape if many else [shape]
    types = dtype if isinstance(dtype, tuple) else (dtype,) * len(shapes)
    outs = [jax.ShapeDtypeStruct(s, d) for s, d in zip(shapes, types)]
    return pl.pallas_call(
        kernel,
        out_shape=outs if many else outs[0],
        in_specs=specs,
        out_specs=[VMEM] * len(outs) if many else VMEM,
        scratch_shapes=scratch,
        compiler_params=params(mib),
        input_output_aliases=alias,
        cost_estimate=pl.CostEstimate(flops=cost[0], bytes_accessed=cost[1], transcendentals=0),
    )


def local(
    currents,
    cluster_size,
    radiation,
    receive,
    phase,
    interp,
    trans,
    far_ids,
    far_live,
    near_blocks,
    near_offset,
    near_live,
):
    place = lax.axis_index("clus")
    count = lax.axis_size("clus")

    packed = call(
        pack_kernel, (16, 80, 128), [pltpu.VMEM((1024, 128), F32)], 8, [VMEM] * 3, (1, 2**20)
    )(trans, far_live, far_ids.reshape(8, 128))

    alive = lax.broadcasted_iota(jnp.int32, (32, 128), 1) < cluster_size[:, None]
    own = jnp.where(alive[None, :, None, :], currents, jnp.zeros((), BF))
    own = own.transpose(1, 0, 2, 3).reshape(1, 32, 16, 128)
    copies = jnp.broadcast_to(own, (8, 32, 16, 128))
    alive = jnp.broadcast_to(alive[:, None, :].astype(F32), (32, 16, 128))
    spots = jnp.stack([place, count, lax.axis_index("dir")]).astype(jnp.int32)
    copies, spots = lax.optimization_barrier((copies, spots))
    everyone = lax.all_to_all(copies, "dir", 0, 0)
    across = [(i, i + 1) for i in range(1, count - 1, 2)]
    across = across + [(b, a) for a, b in across]
    own = own.reshape(32, 16, 128)
    met = [
        lax.ppermute(own, ("clus", "dir"), [(a * 8 + i, b * 8 + (i ^ k)) for a, b in across for i in range(8)])
        for k in range(2)
    ]

    up, down = call(
        fold_kernel, [(16, 128, 256), (32, 64, 256)], [], 12, [VMEM] * 3, (2**31, 2**23)
    )(jnp.stack([radiation, receive]), phase, interp[0].T)

    everyone, up, down, packed = lax.optimization_barrier((everyone, up, down, packed))
    rows = pltpu.VMEM((1024, 128), F32)
    parents = call(parents_kernel, (16, 144, 128), [rows], 12, [VMEM] * 3, (2**27, 2**21))(
        everyone, up, packed
    )
    partner = lax.ppermute(everyone, "clus", [(i, i ^ 1) for i in range(count)])
    parents, met = lax.optimization_barrier((parents, met))
    far0 = call(pair_kernel, (2, 32, 16, 128), [], 4, [VMEM] * 2, (1, 2**20))(*met)
    far1, far2, far3 = (
        lax.ppermute(far0, "dir", [(i, (i + 2 * k) % 8) for i in range(8)]) for k in (1, 2, 3)
    )
    sources = lax.all_to_all(parents, "clus", 0, 0)
    translated = call(
        translate_kernel,
        (16, 64, 128),
        [
            pltpu.VMEM((1024, 128), F32),
            pltpu.VMEM((128, 128), F32),
            pltpu.VMEM((2, 2048, 128), F32),
        ],
        12,
        [VMEM],
        (2**32, 2**23),
    )(sources)
    back = lax.all_to_all(translated, "clus", 0, 0)
    near = call(
        near_kernel,
        (32, 128, 128),
        [pltpu.VMEM((8, 32, 16, 128), BF)],
        12,
        [SMEM] * 3 + [VMEM] * 7,
        (2**30, 2**23),
    )(spots, near_offset.T, near_live.T, everyone, partner, far0, far1, far2, far3, near_blocks)
    partial = call(far_kernel, (8, 32, 16, 128), [rows], 12, [VMEM] * 3, (2**28, 2**22))(
        back, down, near
    )
    shares = lax.all_to_all(partial, "dir", 0, 0)
    return call(total_kernel, (2, 32, 8, 128), [], 8, [VMEM] * 2, (1, 2**21))(shares, alive)


def solution(mesh):
    in_specs = (
        P(None, "clus", "dir", None),
        P("clus"),
        P(None, "clus", "dir", None),
        P(None, "clus", "dir", None),
        P("clus", "dir"),
        P("dir", None, None),
        P(None, "clus", None, "dir"),
        P("clus", None),
        P("clus", None),
        P(None, "clus", "dir", None, None),
        P("clus", "dir"),
        P("clus", "dir"),
    )
    out_specs = P(None, "clus", "dir", None)
    return jax.shard_map(local, mesh=mesh, in_specs=in_specs, out_specs=out_specs, check_vma=False)
```

```python
import jax
import jax.numpy as jnp
from jax import lax
from jax.experimental import pallas as pl
from jax.experimental.pallas import tpu as pltpu
from jax.sharding import PartitionSpec as P

BF = jnp.bfloat16
F32 = jnp.float32
NT = (((1,), (1,)), ((), ()))
NN = (((1,), (0,)), ((), ()))
TN = (((0,), (0,)), ((), ()))
VMEM = pl.BlockSpec(memory_space=pltpu.VMEM)
ANY = pl.BlockSpec(memory_space=pl.ANY)
SMEM = pl.BlockSpec(memory_space=pltpu.SMEM)


def dot(a, b, dims):
    return lax.dot_general(a, b, dims, preferred_element_type=F32)


def params(mib):
    return pltpu.CompilerParams(vmem_limit_bytes=mib * 2**20)


def turn_lanes(x):
    lane = lax.broadcasted_iota(jnp.int32, x.shape, 1)
    return jnp.where(lane % 16 < 8, -pltpu.roll(x, 120, 1), pltpu.roll(x, 8, 1))


def turn_rows(x):
    y = x.reshape(8, 2, 8, x.shape[1])
    return jnp.stack([-y[:, 1], y[:, 0]], axis=1).reshape(x.shape)


def mask_kernel(size, currents, copies, own, alive):
    lane = lax.broadcasted_iota(jnp.int32, (16, 128), 1)
    for c in range(32):
        both = jnp.concatenate([currents[0, c], currents[1, c]], axis=0).astype(F32)
        alive[c] = jnp.where(lane < size[c], 1.0, 0.0)
        both = jnp.where(lane < size[c], both, 0.0).astype(BF)
        own[c] = both
        for d in range(8):
            copies[d, c] = both


def pack_kernel(trans, live, ids, out, rows):
    for pp in range(8):
        for r in range(2):
            tiles = []
            for p in (2 * pp, 2 * pp + 1):
                tile = trans[r, p].astype(F32).T
                tiles.append(jnp.where(live[pl.ds(p, 1), :] == 1, tile, 0.0))
            rows[pl.ds(r * 8 + pp, 64, stride=16), :] = jnp.concatenate(tiles, axis=1)
    out[:, 0:64, :] = rows[...].reshape(16, 64, 128).astype(BF)
    pairs = ids[...].astype(F32)
    pairs = jnp.concatenate([pairs, jnp.zeros((8, 128), F32)], axis=0).astype(BF)
    out[:, 64:80, :] = jnp.broadcast_to(pairs[None], (16, 16, 128))


def translate_kernel(packed, out, rows, ids, sums):
    rows[...] = packed[:, 64:128, :].astype(F32).reshape(1024, 128)
    ids[...] = packed[:, 128:144, :].astype(F32)[:, 0:8, :].reshape(128, 128)
    lane = lax.broadcasted_iota(jnp.int32, (8, 128), 1)
    source = lax.broadcasted_iota(jnp.int32, (128, 128), 1).astype(F32)
    columns = ids[...].T
    none = jnp.zeros((16, 128), BF)
    for i in range(64):
        left, hits = [], []
        for n in range(2):
            k = 2 * i + n
            factors = rows[pl.ds((k // 8) * 64 + k % 8, 8, stride=8), :]
            both = jnp.concatenate(
                [jnp.where(lane < 64, factors, 0.0), jnp.where(lane < 64, 0.0, factors)], axis=0
            ).astype(BF)
            left.append(jnp.concatenate([none] * n + [both] + [none] * (1 - n), axis=1))
            wanted = jnp.broadcast_to(columns[:, k : k + 1], (128, 128))
            halves = [jnp.where(source == wanted - 128.0 * h, 1.0, 0.0).astype(BF) for h in range(2)]
            hits.append(jnp.concatenate(halves, axis=1))
        made = dot(jnp.concatenate(left, axis=0), jnp.concatenate(hits, axis=0), NN)
        for b in range(4):
            for h in range(2):
                sums[h, pl.ds(4 * i + b, 8, stride=256), :] = made[
                    b * 8 : b * 8 + 8, h * 128 : h * 128 + 128
                ]
    for q in range(4):
        src = packed[:, q * 16 : q * 16 + 16, :].reshape(256, 128)
        w = slice(q * 512, q * 512 + 512)
        z = dot(sums[0, w, :].astype(BF), src[0:128], NN) + dot(sums[1, w, :].astype(BF), src[128:256], NN)
        done = z[0:256] + turn_lanes(z[256:512])
        out[:, q * 16 : q * 16 + 16, :] = done.reshape(16, 16, 128).astype(BF)


def fold_kernel(patterns, phase, interp, up, down):
    turned = jnp.concatenate([phase[...], jnp.zeros((32, 64), F32)], axis=1).T[0:64]
    cosine = jnp.cos(turned)
    sine = jnp.sin(turned)
    raise4 = []
    for n in range(4):
        left = [jnp.zeros((32, 64 * n), F32)] if n else []
        right = [jnp.zeros((32, 64 * (3 - n)), F32)] if n < 3 else []
        raise4.append(jnp.concatenate(left + [interp[...]] + right, axis=1))
    raise4 = jnp.concatenate(raise4, axis=0).T.astype(BF)
    for g in range(8):
        sent = [dot(raise4, patterns[0, r, g * 4 : g * 4 + 4].reshape(128, 128), NN) for r in range(2)]
        got = [dot(raise4, patterns[1, r, g * 4 : g * 4 + 4].reshape(128, 128), NN) for r in range(2)]
        for n in range(4):
            c = g * 4 + n
            co = jnp.broadcast_to(cosine[:, c : c + 1], (64, 128))
            si = jnp.broadcast_to(sine[:, c : c + 1], (64, 128))
            ur, ui = (s[n * 64 : n * 64 + 64] for s in sent)
            vr, vi = (s[n * 64 : n * 64 + 64] for s in got)
            b = (c % 2) * 128
            up[c // 2, 0:64, b : b + 128] = (co * ur - si * ui).astype(BF)
            up[c // 2, 64:128, b : b + 128] = (si * ur + co * ui).astype(BF)
            down[c, :, 0:128] = (co * vr + si * vi).astype(BF)
            down[c, :, 128:256] = (co * vi - si * vr).astype(BF)


def pair_kernel(first, second, out):
    out[0] = first[...]
    out[1] = second[...]


def parents_kernel(everyone, up, packed, out, rows):
    out[:, 64:144, :] = packed[...]
    for p in range(16):
        x = jnp.concatenate(
            [everyone[:, 2 * p + b].reshape(128, 128) for b in range(2)], axis=1
        )
        y = dot(up[p], x, NT)
        rows[pl.ds(p, 64, stride=16), :] = y[0:64] + turn_lanes(y[64:128])
    out[:, 0:64, :] = rows[...].reshape(16, 64, 128).astype(BF)


def near_kernel(place, offset, live, own, partner, far0, far1, far2, far3, blocks, out, far, held, ready):
    first = place[0] * 32
    even = place[0] % 2 == 0
    chunks = [
        pltpu.make_async_copy(blocks.at[:, pl.ds(g * 8, 8)], held.at[:, pl.ds(g * 8, 8)], ready.at[g])
        for g in range(4)
    ]
    for copy in chunks:
        copy.start()
    bases = (first, jnp.where(even, first + 32, first - 32), jnp.where(even, first - 32, first + 32))
    for k, part in enumerate((far0, far1, far2, far3)):
        for b in range(2):
            far[2 * ((place[2] // 2 + 4 - k) % 4) + (place[2] + b) % 2] = part[b]

    def step(c, carry):
        picked = []
        for j in range(2):
            source = jnp.clip(first + c + offset[j, c], 0, place[1] * 32 - 1)
            x = jnp.zeros((128, 128), BF)
            for cells, base in zip((own, partner, far), bases):
                spot = source - base
                here = (live[j, c] == 1) & (spot >= 0) & (spot < 32)
                x = jnp.where(here, cells[:, jnp.clip(spot, 0, 31)].reshape(128, 128), x)
            picked.append(x)
        parts = [jnp.concatenate([held[r, c, j] for j in range(2)], axis=1) for r in range(2)]
        y = dot(jnp.concatenate(picked, axis=1), jnp.concatenate(parts, axis=0), NT)
        out[c] = (y[:, 0:128] + turn_rows(y[:, 128:256])).astype(BF)
        return carry

    for g in range(4):
        chunks[g].wait()
        lax.fori_loop(g * 8, g * 8 + 8, step, 0, unroll=4)


def far_kernel(translated, down, near, out, rows):
    rows[...] = translated[...].astype(F32).reshape(1024, 128)
    for p in range(16):
        t = rows[pl.ds(p, 64, stride=16), :].T.astype(BF)
        for c in (2 * p, 2 * p + 1):
            y = dot(t, down[c], NN)
            field = y[:, 0:128] + turn_rows(y[:, 128:256]) + near[c].astype(F32)
            out[:, c] = field.reshape(8, 16, 128).astype(BF)


def total_kernel(shares, alive, out):
    total = shares[0].astype(F32)
    for d in range(1, 8):
        total += shares[d].astype(F32)
    total = jnp.where(alive[...] > 0.0, total, 0.0)
    for r in range(2):
        out[r] = total[:, r * 8 : r * 8 + 8].astype(BF)


def call(kernel, shape, scratch, mib, specs, cost, dtype=BF, alias={}):
    many = isinstance(shape, list)
    shapes = shape if many else [shape]
    types = dtype if isinstance(dtype, tuple) else (dtype,) * len(shapes)
    outs = [jax.ShapeDtypeStruct(s, d) for s, d in zip(shapes, types)]
    return pl.pallas_call(
        kernel,
        out_shape=outs if many else outs[0],
        in_specs=specs,
        out_specs=[VMEM] * len(outs) if many else VMEM,
        scratch_shapes=scratch,
        compiler_params=params(mib),
        input_output_aliases=alias,
        cost_estimate=pl.CostEstimate(flops=cost[0], bytes_accessed=cost[1], transcendentals=0),
    )


def local(
    currents,
    cluster_size,
    radiation,
    receive,
    phase,
    interp,
    trans,
    far_ids,
    far_live,
    near_blocks,
    near_offset,
    near_live,
):
    place = lax.axis_index("clus")
    count = lax.axis_size("clus")

    packed = call(
        pack_kernel, (16, 80, 128), [pltpu.VMEM((1024, 128), F32)], 8, [VMEM] * 3, (1, 2**20)
    )(trans, far_live, far_ids.reshape(8, 128))

    copies, own, alive = call(
        mask_kernel,
        [(8, 32, 16, 128), (32, 16, 128), (32, 16, 128)],
        [],
        60,
        [SMEM, VMEM],
        (1, 2**21),
        (BF, BF, F32),
    )(cluster_size, currents)
    across = [(i, i + 1) for i in range(1, count - 1, 2)]
    across = across + [(b, a) for a, b in across]
    met = [
        lax.ppermute(own, ("clus", "dir"), [(a * 8 + i, b * 8 + (i ^ k)) for a, b in across for i in range(8)])
        for k in range(2)
    ]
    spots = jnp.stack([place, count, lax.axis_index("dir")]).astype(jnp.int32)
    copies, spots = lax.optimization_barrier((copies, spots))
    everyone = lax.all_to_all(copies, "dir", 0, 0)
    across = [(i, i + 1) for i in range(1, count - 1, 2)]
    across = across + [(b, a) for a, b in across]
    own = own.reshape(32, 16, 128)
    met = [
        lax.ppermute(own, ("clus", "dir"), [(a * 8 + i, b * 8 + (i ^ k)) for a, b in across for i in range(8)])
        for k in range(2)
    ]

    up, down = call(
        fold_kernel, [(16, 128, 256), (32, 64, 256)], [], 12, [VMEM] * 3, (2**31, 2**23)
    )(jnp.stack([radiation, receive]), phase, interp[0].T)

    everyone, up, down, packed = lax.optimization_barrier((everyone, up, down, packed))
    rows = pltpu.VMEM((1024, 128), F32)
    parents = call(parents_kernel, (16, 144, 128), [rows], 12, [VMEM] * 3, (2**27, 2**21))(
        everyone, up, packed
    )
    partner = lax.ppermute(everyone, "clus", [(i, i ^ 1) for i in range(count)])
    parents, met = lax.optimization_barrier((parents, met))
    far0 = call(pair_kernel, (2, 32, 16, 128), [], 4, [VMEM] * 2, (1, 2**20))(*met)
    far1, far2, far3 = (
        lax.ppermute(far0, "dir", [(i, (i + 2 * k) % 8) for i in range(8)]) for k in (1, 2, 3)
    )
    sources = lax.all_to_all(parents, "clus", 0, 0)
    translated = call(
        translate_kernel,
        (16, 64, 128),
        [
            pltpu.VMEM((1024, 128), F32),
            pltpu.VMEM((128, 128), F32),
            pltpu.VMEM((2, 2048, 128), F32),
        ],
        12,
        [VMEM],
        (2**32, 2**23),
    )(sources)
    back = lax.all_to_all(translated, "clus", 0, 0)
    near = call(
        near_kernel,
        (32, 128, 128),
        [
            pltpu.VMEM((8, 32, 16, 128), BF),
            pltpu.VMEM((2, 32, 2, 128, 128), BF),
            pltpu.SemaphoreType.DMA((4,)),
        ],
        58,
        [SMEM] * 3 + [VMEM] * 6 + [ANY],
        (2**30, 2**23),
    )(spots, near_offset.T, near_live.T, everyone, partner, far0, far1, far2, far3, near_blocks)
    partial = call(far_kernel, (8, 32, 16, 128), [rows], 12, [VMEM] * 3, (2**28, 2**22))(
        back, down, near
    )
    shares = lax.all_to_all(partial, "dir", 0, 0)
    return call(total_kernel, (2, 32, 8, 128), [], 8, [VMEM] * 2, (1, 2**21))(shares, alive)


def solution(mesh):
    in_specs = (
        P(None, "clus", "dir", None),
        P("clus"),
        P(None, "clus", "dir", None),
        P(None, "clus", "dir", None),
        P("clus", "dir"),
        P("dir", None, None),
        P(None, "clus", None, "dir"),
        P("clus", None),
        P("clus", None),
        P(None, "clus", "dir", None, None),
        P("clus", "dir"),
        P("clus", "dir"),
    )
    out_specs = P(None, "clus", "dir", None)
    return jax.shard_map(local, mesh=mesh, in_specs=in_specs, out_specs=out_specs, check_vma=False)
```

```python
import jax
import jax.numpy as jnp
from jax import lax
from jax.experimental import pallas as pl
from jax.experimental.pallas import tpu as pltpu
from jax.sharding import PartitionSpec as P

BF = jnp.bfloat16
F32 = jnp.float32
NT = (((1,), (1,)), ((), ()))
NN = (((1,), (0,)), ((), ()))
TN = (((0,), (0,)), ((), ()))
VMEM = pl.BlockSpec(memory_space=pltpu.VMEM)
ANY = pl.BlockSpec(memory_space=pl.ANY)
SMEM = pl.BlockSpec(memory_space=pltpu.SMEM)


def dot(a, b, dims):
    return lax.dot_general(a, b, dims, preferred_element_type=F32)


def params(mib):
    return pltpu.CompilerParams(vmem_limit_bytes=mib * 2**20)


def turn_lanes(x):
    lane = lax.broadcasted_iota(jnp.int32, x.shape, 1)
    return jnp.where(lane % 16 < 8, -pltpu.roll(x, 120, 1), pltpu.roll(x, 8, 1))


def turn_rows(x):
    y = x.reshape(8, 2, 8, x.shape[1])
    return jnp.stack([-y[:, 1], y[:, 0]], axis=1).reshape(x.shape)


def mask_kernel(size, currents, copies, own, alive):
    lane = lax.broadcasted_iota(jnp.int32, (16, 128), 1)
    for c in range(32):
        both = jnp.concatenate([currents[0, c], currents[1, c]], axis=0).astype(F32)
        alive[c] = jnp.where(lane < size[c], 1.0, 0.0)
        both = jnp.where(lane < size[c], both, 0.0).astype(BF)
        own[c] = both
        for d in range(8):
            copies[d, c] = both


def pack_kernel(trans, live, ids, out, rows):
    for pp in range(8):
        for r in range(2):
            tiles = []
            for p in (2 * pp, 2 * pp + 1):
                tile = trans[r, p].astype(F32).T
                tiles.append(jnp.where(live[pl.ds(p, 1), :] == 1, tile, 0.0))
            rows[pl.ds(r * 8 + pp, 64, stride=16), :] = jnp.concatenate(tiles, axis=1)
    out[:, 0:64, :] = rows[...].reshape(16, 64, 128).astype(BF)
    pairs = ids[...].astype(F32)
    pairs = jnp.concatenate([pairs, jnp.zeros((8, 128), F32)], axis=0).astype(BF)
    out[:, 64:80, :] = jnp.broadcast_to(pairs[None], (16, 16, 128))


def translate_kernel(packed, out, rows, ids, sums):
    rows[...] = packed[:, 64:128, :].astype(F32).reshape(1024, 128)
    ids[...] = packed[:, 128:144, :].astype(F32)[:, 0:8, :].reshape(128, 128)
    lane = lax.broadcasted_iota(jnp.int32, (8, 128), 1)
    source = lax.broadcasted_iota(jnp.int32, (128, 128), 1).astype(F32)
    columns = ids[...].T
    none = jnp.zeros((16, 128), BF)
    for i in range(64):
        left, hits = [], []
        for n in range(2):
            k = 2 * i + n
            factors = rows[pl.ds((k // 8) * 64 + k % 8, 8, stride=8), :]
            both = jnp.concatenate(
                [jnp.where(lane < 64, factors, 0.0), jnp.where(lane < 64, 0.0, factors)], axis=0
            ).astype(BF)
            left.append(jnp.concatenate([none] * n + [both] + [none] * (1 - n), axis=1))
            wanted = jnp.broadcast_to(columns[:, k : k + 1], (128, 128))
            halves = [jnp.where(source == wanted - 128.0 * h, 1.0, 0.0).astype(BF) for h in range(2)]
            hits.append(jnp.concatenate(halves, axis=1))
        made = dot(jnp.concatenate(left, axis=0), jnp.concatenate(hits, axis=0), NN)
        for b in range(4):
            for h in range(2):
                sums[h, pl.ds(4 * i + b, 8, stride=256), :] = made[
                    b * 8 : b * 8 + 8, h * 128 : h * 128 + 128
                ]
    for q in range(4):
        src = packed[:, q * 16 : q * 16 + 16, :].reshape(256, 128)
        w = slice(q * 512, q * 512 + 512)
        z = dot(sums[0, w, :].astype(BF), src[0:128], NN) + dot(sums[1, w, :].astype(BF), src[128:256], NN)
        done = z[0:256] + turn_lanes(z[256:512])
        out[:, q * 16 : q * 16 + 16, :] = done.reshape(16, 16, 128).astype(BF)


def fold_kernel(patterns, phase, interp, up, down):
    turned = jnp.concatenate([phase[...], jnp.zeros((32, 64), F32)], axis=1).T[0:64]
    cosine = jnp.cos(turned)
    sine = jnp.sin(turned)
    raise4 = []
    for n in range(4):
        left = [jnp.zeros((32, 64 * n), F32)] if n else []
        right = [jnp.zeros((32, 64 * (3 - n)), F32)] if n < 3 else []
        raise4.append(jnp.concatenate(left + [interp[...]] + right, axis=1))
    raise4 = jnp.concatenate(raise4, axis=0).T.astype(BF)
    for g in range(8):
        sent = [dot(raise4, patterns[0, r, g * 4 : g * 4 + 4].reshape(128, 128), NN) for r in range(2)]
        got = [dot(raise4, patterns[1, r, g * 4 : g * 4 + 4].reshape(128, 128), NN) for r in range(2)]
        for n in range(4):
            c = g * 4 + n
            co = jnp.broadcast_to(cosine[:, c : c + 1], (64, 128))
            si = jnp.broadcast_to(sine[:, c : c + 1], (64, 128))
            ur, ui = (s[n * 64 : n * 64 + 64] for s in sent)
            vr, vi = (s[n * 64 : n * 64 + 64] for s in got)
            b = (c % 2) * 128
            up[c // 2, 0:64, b : b + 128] = (co * ur - si * ui).astype(BF)
            up[c // 2, 64:128, b : b + 128] = (si * ur + co * ui).astype(BF)
            down[c, :, 0:128] = (co * vr + si * vi).astype(BF)
            down[c, :, 128:256] = (co * vi - si * vr).astype(BF)


def pair_kernel(first, second, out):
    out[0] = first[...]
    out[1] = second[...]


def parents_kernel(everyone, up, packed, out, rows):
    out[:, 64:144, :] = packed[...]
    for p in range(16):
        x = jnp.concatenate(
            [everyone[:, 2 * p + b].reshape(128, 128) for b in range(2)], axis=1
        )
        y = dot(up[p], x, NT)
        rows[pl.ds(p, 64, stride=16), :] = y[0:64] + turn_lanes(y[64:128])
    out[:, 0:64, :] = rows[...].reshape(16, 64, 128).astype(BF)


def near_kernel(place, offset, live, own, partner, far0, far1, far2, far3, blocks, out, far, held, ready):
    first = place[0] * 32
    even = place[0] % 2 == 0
    chunks = [
        pltpu.make_async_copy(blocks.at[:, pl.ds(g * 8, 8)], held.at[:, pl.ds(g * 8, 8)], ready.at[g])
        for g in range(4)
    ]
    for copy in chunks:
        copy.start()
    bases = (first, jnp.where(even, first + 32, first - 32), jnp.where(even, first - 32, first + 32))
    for k, part in enumerate((far0, far1, far2, far3)):
        for b in range(2):
            far[2 * ((place[2] // 2 + 4 - k) % 4) + (place[2] + b) % 2] = part[b]

    def step(c, carry):
        picked = []
        for j in range(2):
            source = jnp.clip(first + c + offset[j, c], 0, place[1] * 32 - 1)
            x = jnp.zeros((128, 128), BF)
            for cells, base in zip((own, partner, far), bases):
                spot = source - base
                here = (live[j, c] == 1) & (spot >= 0) & (spot < 32)
                x = jnp.where(here, cells[:, jnp.clip(spot, 0, 31)].reshape(128, 128), x)
            picked.append(x)
        parts = [jnp.concatenate([held[r, c, j] for j in range(2)], axis=1) for r in range(2)]
        y = dot(jnp.concatenate(picked, axis=1), jnp.concatenate(parts, axis=0), NT)
        out[c] = (y[:, 0:128] + turn_rows(y[:, 128:256])).astype(BF)
        return carry

    for g in range(4):
        chunks[g].wait()
        lax.fori_loop(g * 8, g * 8 + 8, step, 0, unroll=4)


def far_kernel(translated, down, near, out, rows):
    rows[...] = translated[...].astype(F32).reshape(1024, 128)
    for p in range(16):
        t = rows[pl.ds(p, 64, stride=16), :].T.astype(BF)
        for c in (2 * p, 2 * p + 1):
            y = dot(t, down[c], NN)
            field = y[:, 0:128] + turn_rows(y[:, 128:256]) + near[c].astype(F32)
            out[:, c] = field.reshape(8, 16, 128).astype(BF)


def total_kernel(shares, alive, out):
    total = shares[0].astype(F32)
    for d in range(1, 8):
        total += shares[d].astype(F32)
    total = jnp.where(alive[...] > 0.0, total, 0.0)
    for r in range(2):
        out[r] = total[:, r * 8 : r * 8 + 8].astype(BF)


def call(kernel, shape, scratch, mib, specs, cost, dtype=BF, alias={}):
    many = isinstance(shape, list)
    shapes = shape if many else [shape]
    types = dtype if isinstance(dtype, tuple) else (dtype,) * len(shapes)
    outs = [jax.ShapeDtypeStruct(s, d) for s, d in zip(shapes, types)]
    return pl.pallas_call(
        kernel,
        out_shape=outs if many else outs[0],
        in_specs=specs,
        out_specs=[VMEM] * len(outs) if many else VMEM,
        scratch_shapes=scratch,
        compiler_params=params(mib),
        input_output_aliases=alias,
        cost_estimate=pl.CostEstimate(flops=cost[0], bytes_accessed=cost[1], transcendentals=0),
    )


def local(
    currents,
    cluster_size,
    radiation,
    receive,
    phase,
    interp,
    trans,
    far_ids,
    far_live,
    near_blocks,
    near_offset,
    near_live,
):
    place = lax.axis_index("clus")
    count = lax.axis_size("clus")

    packed = call(
        pack_kernel, (16, 80, 128), [pltpu.VMEM((1024, 128), F32)], 8, [VMEM] * 3, (1, 2**20)
    )(trans, far_live, far_ids.reshape(8, 128))

    copies, own, alive = call(
        mask_kernel,
        [(8, 32, 16, 128), (32, 16, 128), (32, 16, 128)],
        [],
        60,
        [SMEM, VMEM],
        (1, 2**21),
        (BF, BF, F32),
    )(cluster_size, currents)
    across = [(i, i + 1) for i in range(1, count - 1, 2)]
    across = across + [(b, a) for a, b in across]
    met = [
        lax.ppermute(own, ("clus", "dir"), [(a * 8 + i, b * 8 + (i ^ k)) for a, b in across for i in range(8)])
        for k in range(2)
    ]
    spots = jnp.stack([place, count, lax.axis_index("dir")]).astype(jnp.int32)
    everyone = lax.all_to_all(copies, "dir", 0, 0)
    across = [(i, i + 1) for i in range(1, count - 1, 2)]
    across = across + [(b, a) for a, b in across]
    own = own.reshape(32, 16, 128)
    met = [
        lax.ppermute(own, ("clus", "dir"), [(a * 8 + i, b * 8 + (i ^ k)) for a, b in across for i in range(8)])
        for k in range(2)
    ]

    up, down = call(
        fold_kernel, [(16, 128, 256), (32, 64, 256)], [], 12, [VMEM] * 3, (2**31, 2**23)
    )(jnp.stack([radiation, receive]), phase, interp[0].T)

    everyone, up, down, packed, spots = lax.optimization_barrier(
        (everyone, up, down, packed, spots)
    )
    rows = pltpu.VMEM((1024, 128), F32)
    parents = call(parents_kernel, (16, 144, 128), [rows], 12, [VMEM] * 3, (2**27, 2**21))(
        everyone, up, packed
    )
    partner = lax.ppermute(everyone, "clus", [(i, i ^ 1) for i in range(count)])
    parents, met = lax.optimization_barrier((parents, met))
    far0 = call(pair_kernel, (2, 32, 16, 128), [], 4, [VMEM] * 2, (1, 2**20))(*met)
    far1, far2, far3 = (
        lax.ppermute(far0, "dir", [(i, (i + 2 * k) % 8) for i in range(8)]) for k in (1, 2, 3)
    )
    sources = lax.all_to_all(parents, "clus", 0, 0)
    translated = call(
        translate_kernel,
        (16, 64, 128),
        [
            pltpu.VMEM((1024, 128), F32),
            pltpu.VMEM((128, 128), F32),
            pltpu.VMEM((2, 2048, 128), F32),
        ],
        12,
        [VMEM],
        (2**32, 2**23),
    )(sources)
    back = lax.all_to_all(translated, "clus", 0, 0)
    near = call(
        near_kernel,
        (32, 128, 128),
        [
            pltpu.VMEM((8, 32, 16, 128), BF),
            pltpu.VMEM((2, 32, 2, 128, 128), BF),
            pltpu.SemaphoreType.DMA((4,)),
        ],
        58,
        [SMEM] * 3 + [VMEM] * 6 + [ANY],
        (2**30, 2**23),
    )(spots, near_offset.T, near_live.T, everyone, partner, far0, far1, far2, far3, near_blocks)
    partial = call(far_kernel, (8, 32, 16, 128), [rows], 12, [VMEM] * 3, (2**28, 2**22))(
        back, down, near
    )
    shares = lax.all_to_all(partial, "dir", 0, 0)
    return call(total_kernel, (2, 32, 8, 128), [], 8, [VMEM] * 2, (1, 2**21))(shares, alive)


def solution(mesh):
    in_specs = (
        P(None, "clus", "dir", None),
        P("clus"),
        P(None, "clus", "dir", None),
        P(None, "clus", "dir", None),
        P("clus", "dir"),
        P("dir", None, None),
        P(None, "clus", None, "dir"),
        P("clus", None),
        P("clus", None),
        P(None, "clus", "dir", None, None),
        P("clus", "dir"),
        P("clus", "dir"),
    )
    out_specs = P(None, "clus", "dir", None)
    return jax.shard_map(local, mesh=mesh, in_specs=in_specs, out_specs=out_specs, check_vma=False)
```
